32 devices in a mesh: req: 8 (over z, y), kvh: 4 (over x, core).
Axes of the slice: x: 2, y: 2, z: 4, core: 2. Of those that a mesh axis runs over, the one named last changes fastest.
Arguments:
- queries: bfloat16 [512, 4, 8, 128], P('req', 'kvh')
- key_cache: bfloat16 [1280, 4, 128, 128], P('req', 'kvh')
- value_cache: bfloat16 [1280, 4, 128, 128], P('req', 'kvh'), may hold values from -24 to 24
- lengths: int32 [512], P('req'), may hold values from 1 to 4096, as said below
- page_table: int32 [512, 32], P('req'), may hold values from 0 to 159, as said below
- residual_in: bfloat16 [512, 2048], P(('req', 'kvh')), may hold values from -4 to 4
- w_out: bfloat16 [4096, 2048], P('kvh'), may hold values from -0.09375 to 0.09375
- norm_gain: bfloat16 [2048], replicated, may hold values from 0.099609375 to 1.8984375
- route_logits: float32 [512, 8], P(('req', 'kvh'))
- routes: int32 [512, 8], P(('req', 'kvh')), may hold values from 0 to 31, as said below
- w_gate: bfloat16 [32, 2048, 768], P(('req', 'kvh')), may hold values from -0.125 to 0.125
- w_up: bfloat16 [32, 2048, 768], P(('req', 'kvh')), may hold values from -0.125 to 0.125
- w_down: bfloat16 [32, 768, 2048], P(('req', 'kvh')), may hold values from -0.21875 to 0.21875
Outputs:
- layer_out: bfloat16 [512, 2048], P(('req', 'kvh'))
The draws below stay inside these ranges and needn't reach their ends.
Inputs may be any that keep to these rules, and one draw needn't show every extreme that they name: `lengths`: every request of a block of 64 has between 1 and 32 pages; some request reaches 4096. `page_table`: local page numbers within the pool of the request's block of 64 requests. Entries 0 to ceil(lengths / 128) - 1 of the requests of one block are all distinct; later entries repeat the request's last used page. `routes`: each token names 8 different experts. Of the 16 tokens of one device, at most 8 name the same expert, and some expert is named by exactly 8 tokens of every device.
All inputs are finite; a program needn't handle non-finite values.
Results may differ from the reference program's by a relative error of at most 0.0054.
Values may be sent and summed in bfloat16 or wider, within the bound.
A program may use at most 192 MiB of HBM per device.

```python
import jax
import jax.numpy as jnp
from jax import lax

D = 2048
H = 32
KVH = 4
HD = 128
FF = 768
TOP = 8
PAGE = 128
REQ_DEV = 64
G = 8
MAXP = 32
PAGES_DEV = 160
PAGES = 1280
REQUESTS = 512
TOK_DEV = 16
TOKENS = 512
EXPERTS = 32
CAP = 8
N_REQ = 8


def cache_layout(key):
    base_key = jax.random.fold_in(key, 101)
    level_key, order_key, tail_key, pool_key = jax.random.split(base_key, 4)
    levels = jax.random.randint(level_key, (N_REQ,), 0, 4).astype(jnp.int32)
    levels = levels.at[0].set(0)
    extra_pages = jnp.right_shift(jnp.full((N_REQ,), PAGES_DEV - REQ_DEV, jnp.int32), levels)
    orders = jax.vmap(lambda block_key: jax.random.permutation(block_key, REQ_DEV))(jax.random.split(order_key, N_REQ))
    rank_in_block = jnp.argsort(orders, axis=1).astype(jnp.int32)
    page_counts = 1 + jnp.clip(extra_pages[:, None] - (MAXP - 1) * rank_in_block, 0, MAXP - 1)
    last_fill = jax.random.randint(tail_key, (N_REQ, REQ_DEV), 1, PAGE + 1).astype(jnp.int32)
    last_fill = jnp.where(page_counts == MAXP, PAGE, last_fill)
    lengths = ((page_counts - 1) * PAGE + last_fill).astype(jnp.int32)
    page_orders = jax.vmap(lambda block_key: jax.random.permutation(block_key, PAGES_DEV))(jax.random.split(pool_key, N_REQ)).astype(jnp.int32)
    offsets = jnp.cumsum(page_counts, axis=1) - page_counts
    columns = jnp.arange(MAXP, dtype=jnp.int32)
    page_spots = offsets[:, :, None] + jnp.minimum(columns[None, None, :], page_counts[:, :, None] - 1)
    page_table = jax.vmap(lambda order_row, spot_rows: order_row[spot_rows])(page_orders, page_spots).astype(jnp.int32)
    return (lengths, page_table)


def key_field_draw(key):
    base_key = jax.random.fold_in(key, 211)
    noise_key, scale_key = jax.random.split(base_key, 2)
    shape = (PAGES, KVH, PAGE, HD)
    values = jax.random.normal(noise_key, shape, jnp.float32)
    spread = jnp.exp(jax.random.uniform(scale_key, (PAGES, KVH, PAGE, 1), jnp.float32, jnp.log(0.3), jnp.log(3.0)))
    key_field = values * spread
    return key_field


def draw_lengths(key, part):
    lengths, page_table = cache_layout(key)
    return lengths.reshape(REQUESTS)


def draw_page_table(key, part):
    lengths, page_table = cache_layout(key)
    return page_table.reshape(REQUESTS, MAXP)


def draw_key_cache(key, part):
    key_field = key_field_draw(key)
    return key_field.astype(jnp.bfloat16)


def draw_queries(key, part):
    base_key = jax.random.fold_in(key, 231)
    noise_key, scale_key = jax.random.split(base_key, 2)
    shape = (REQUESTS, KVH, G, HD)
    values = jax.random.normal(noise_key, shape, jnp.float32)
    spread = jnp.exp(jax.random.uniform(scale_key, (REQUESTS, KVH, G, 1), jnp.float32, jnp.log(0.15), jnp.log(1.5)))
    result = values * spread
    return result.astype(jnp.bfloat16)


def draw_route_logits(key, part):
    base_key = jax.random.fold_in(key, 311)
    noise_key, scale_key = jax.random.split(base_key, 2)
    spread = jnp.exp(jax.random.uniform(scale_key, (TOKENS, 1), jnp.float32, jnp.log(0.4), jnp.log(4.0)))
    values = jax.random.normal(noise_key, (TOKENS, TOP), jnp.float32) * spread
    return values


def draw_routes(key, part):
    base_key = jax.random.fold_in(key, 401)
    weight_key, hot_key, pick_key, shuffle_key = jax.random.split(base_key, 4)
    expert_boost = jnp.left_shift(jnp.ones((EXPERTS,), jnp.int32), jax.random.randint(weight_key, (EXPERTS,), 0, 3).astype(jnp.int32))
    hot_expert = jax.random.randint(hot_key, (), 0, EXPERTS).astype(jnp.int32)
    slot_ids = jnp.arange(EXPERTS * CAP, dtype=jnp.int32)
    slot_owner = slot_ids // CAP

    def block_routes(block_key):
        priority = jax.random.randint(block_key, (EXPERTS * CAP,), 0, 4096).astype(jnp.int32) * expert_boost[slot_owner]
        slot_score = priority * (EXPERTS * CAP) + slot_ids
        slot_score = jnp.where(slot_owner == hot_expert, (1 << 28) + slot_ids, slot_score)
        ignored, chosen = lax.top_k(slot_score, TOK_DEV * TOP)
        ordered = jnp.sort(chosen.astype(jnp.int32)) // CAP
        return ordered.reshape(TOP, TOK_DEV).T
    blocks = TOKENS // TOK_DEV
    picked = jax.vmap(block_routes)(jax.random.split(pick_key, blocks)).reshape(TOKENS, TOP)
    orders = jax.vmap(lambda token_key: jax.random.permutation(token_key, TOP))(jax.random.split(shuffle_key, TOKENS)).astype(jnp.int32)
    return jnp.take_along_axis(picked, orders, axis=1).astype(jnp.int32)


def level_of(rng, shape, cuts, smallest, top_value):
    factor_of, own = 1.0, jax.random.fold_in(rng, 6)
    for dim, parts in cuts:
        heights = jnp.exp(jax.random.uniform(jax.random.fold_in(own, dim), (parts,), jnp.float32, smallest / len(cuts), top_value / len(cuts)))
        factor_of = factor_of * jnp.repeat(heights, shape[dim] // parts).reshape([-1 if axis == dim else 1 for axis in range(len(shape))])
    return factor_of


def gaussian(key, shape, scale, most, shards=(), kind=jnp.bfloat16):
    loudness = level_of(key, shape, shards, -0.22, 0.18) if shards else 1.0
    values = jax.random.normal(key, shape, jnp.float32) * scale * loudness
    return jnp.minimum(jnp.maximum(values, -most), most).astype(kind)


def setup_inputs(seed: int = 0) -> dict:
    arg_keys = jax.random.split(jax.random.key(seed), 14)
    queries = draw_queries(jax.random.fold_in(arg_keys[13], 71), 0)
    key_cache = draw_key_cache(jax.random.fold_in(arg_keys[13], 71), 0)
    value_cache = gaussian(arg_keys[2], (PAGES, KVH, PAGE, HD), 4.0, 24.0, ((0, 8), (1, 4)))
    lengths = draw_lengths(jax.random.fold_in(arg_keys[13], 71), 0)
    page_table = draw_page_table(jax.random.fold_in(arg_keys[13], 71), 0)
    residual_in = gaussian(arg_keys[5], (TOKENS, D), 0.5, 4.0, ((0, 32),))
    w_out = gaussian(arg_keys[6], (H * HD, D), (H * HD) ** -0.5, 0.09375, ((0, 4),))
    norm_gain = jnp.clip(1.0 + 0.18 * jax.random.normal(arg_keys[7], (D,), jnp.float32), 0.099609375, 1.8984375).astype(jnp.bfloat16)
    route_logits = draw_route_logits(jax.random.fold_in(arg_keys[13], 71), 0)
    routes = draw_routes(jax.random.fold_in(arg_keys[13], 71), 0)
    w_gate = gaussian(arg_keys[10], (EXPERTS, D, FF), D ** -0.5, 0.125, ((0, 32),))
    w_up = gaussian(arg_keys[11], (EXPERTS, D, FF), D ** -0.5, 0.125, ((0, 32),))
    w_down = gaussian(arg_keys[12], (EXPERTS, FF, D), FF ** -0.5, 0.21875, ((0, 32),))
    return {"queries": queries, "key_cache": key_cache, "value_cache": value_cache, "lengths": lengths, "page_table": page_table, "residual_in": residual_in, "w_out": w_out, "norm_gain": norm_gain, "route_logits": route_logits, "routes": routes, "w_gate": w_gate, "w_up": w_up, "w_down": w_down}


def swish_gate(gate_part, up_part):
    return gate_part / (1.0 + jnp.exp(-gate_part)) * up_part

def usable_slots(lengths, page_table):
    used_pages = (lengths + PAGE - 1) // PAGE
    columns = jnp.arange(MAXP, dtype=jnp.int32)
    pool_ids = jnp.arange(PAGES_DEV, dtype=jnp.int32)
    matched = (page_table[:, :, None] == pool_ids[None, None, :]) & (columns[None, :, None] < used_pages[:, None, None])
    owned_page = jnp.any(matched, axis=1)
    first_pos = lax.optimization_barrier(jnp.sum(jnp.where(matched, columns[None, :, None] * PAGE, 0), axis=1)).astype(jnp.int32)
    offsets = jnp.arange(PAGE, dtype=jnp.int32)
    position = first_pos[:, :, None] + offsets[None, None, :]
    usable = owned_page[:, :, None] & (position < lengths[:, None, None])
    return usable.reshape(lengths.shape[0], PAGES_DEV * PAGE)

def attend_block(operands):
    queries, key_cache, value_cache, lengths, page_table = operands
    usable = usable_slots(lengths, page_table)
    key_flat = jnp.transpose(key_cache, (1, 0, 2, 3)).reshape(KVH, PAGES_DEV * PAGE, HD).astype(jnp.float32)
    value_flat = jnp.transpose(value_cache, (1, 0, 2, 3)).reshape(KVH, PAGES_DEV * PAGE, HD).astype(jnp.float32)
    scores = jnp.einsum('rhgd,hkd->rhgk', queries.astype(jnp.float32), key_flat) * HD ** (-0.5)
    key_mask = usable[:, None, None, :]
    row_max = lax.optimization_barrier(jnp.max(jnp.where(key_mask, scores, -jnp.inf), axis=-1, keepdims=True))
    weights = jnp.where(key_mask, jnp.exp(scores - row_max), 0.0)
    denominator = lax.optimization_barrier(jnp.sum(weights, axis=-1, keepdims=True))
    rounded = lax.optimization_barrier(weights.astype(jnp.bfloat16))
    mixed_values = jnp.einsum('rhgk,hkd->rhgd', rounded.astype(jnp.float32), value_flat)
    return (mixed_values / denominator).astype(jnp.bfloat16)

def earlier_count(pair_routes):
    positions = jnp.arange(pair_routes.shape[0], dtype=jnp.int32)
    same_expert = pair_routes[:, None] == pair_routes[None, :]
    before = positions[None, :] < positions[:, None]
    return lax.optimization_barrier(jnp.sum(same_expert & before, axis=1)).astype(jnp.int32)

def reference(queries, key_cache, value_cache, lengths, page_table, residual_in, w_out, norm_gain, route_logits, routes, w_gate, w_up, w_down):
    attended = lax.map(attend_block, (queries.reshape(N_REQ, REQ_DEV, KVH, G, HD), key_cache.reshape(N_REQ, PAGES_DEV, KVH, PAGE, HD), value_cache.reshape(N_REQ, PAGES_DEV, KVH, PAGE, HD), lengths.reshape(N_REQ, REQ_DEV), page_table.reshape(N_REQ, REQ_DEV, MAXP)))
    attended = attended.reshape(REQUESTS, KVH * G * HD)
    stream = residual_in.astype(jnp.float32) + jnp.dot(attended, w_out, preferred_element_type=jnp.float32)
    inverse_rms = lax.rsqrt(lax.optimization_barrier(jnp.mean(stream * stream, axis=-1, keepdims=True)) + 1e-06)
    normed = (stream * inverse_rms * norm_gain.astype(jnp.float32)).astype(jnp.bfloat16)
    logit_max = lax.optimization_barrier(jnp.max(route_logits, axis=-1, keepdims=True))
    logit_exp = jnp.exp(route_logits - logit_max)
    gate_weights = logit_exp / lax.optimization_barrier(jnp.sum(logit_exp, axis=-1, keepdims=True))
    device_count = EXPERTS
    pair_routes = routes.reshape(device_count, TOK_DEV * TOP)
    pair_slots = jax.vmap(earlier_count)(pair_routes)
    token_routes = pair_routes.reshape(device_count, TOK_DEV, TOP)
    token_slots = pair_slots.reshape(device_count, TOK_DEV, TOP)
    normed_blocks = normed.reshape(device_count, TOK_DEV, D)
    cap_ids = jnp.arange(CAP, dtype=jnp.int32)

    def run_expert(expert_index):
        picked = jnp.any((token_routes[:, None, :, :] == expert_index) & (token_slots[:, None, :, :] == cap_ids[None, :, None, None]), axis=-1)
        gathered = jnp.einsum('bct,btd->bcd', picked.astype(jnp.float32), normed_blocks.astype(jnp.float32)).astype(jnp.bfloat16)
        flat_rows = gathered.reshape(device_count * CAP, D)
        gate_part = jnp.dot(flat_rows, w_gate[expert_index], preferred_element_type=jnp.float32)
        up_part = jnp.dot(flat_rows, w_up[expert_index], preferred_element_type=jnp.float32)
        hidden = swish_gate(gate_part, up_part).astype(jnp.bfloat16)
        produced = jnp.dot(hidden, w_down[expert_index], preferred_element_type=jnp.float32).astype(jnp.bfloat16)
        return produced.reshape(device_count, CAP, D)
    outputs = lax.map(run_expert, jnp.arange(EXPERTS, dtype=jnp.int32))
    block_ids = jnp.broadcast_to(jnp.arange(device_count, dtype=jnp.int32)[:, None], pair_routes.shape)
    fetched = outputs[pair_routes, block_ids, pair_slots].astype(jnp.float32).reshape(TOKENS, TOP, D)
    mixture = lax.optimization_barrier(jnp.sum(gate_weights[:, :, None] * fetched, axis=1))
    return (stream + mixture).astype(jnp.bfloat16)
```

```python
import functools

import jax
import jax.numpy as jnp
from jax import lax
from jax.experimental import pallas as pl
from jax.experimental.pallas import tpu as pltpu
from jax.sharding import PartitionSpec as P

MESH = pl.DeviceIdType.MESH


def swish_gate(gate_part, up_part):
    return gate_part / (1.0 + jnp.exp(-gate_part)) * up_part


def page_owners(lengths, page_table, pool_pages, page_slots):
    entry_count = page_table.shape[1]
    columns = jnp.arange(entry_count, dtype=jnp.int32)
    pool_ids = jnp.arange(pool_pages, dtype=jnp.int32)
    room = lengths[:, None] - columns[None, :] * page_slots
    counts = jnp.clip(room, 0, page_slots)
    matched = page_table[:, :, None] == pool_ids[None, None, :]
    fill = jnp.sum(jnp.where(matched, counts[:, :, None], 0), axis=1)
    return fill > 0, jnp.sum(fill, axis=0)


def page_kernel(scale, filled_ref, query_ref, key_ref, value_ref, top_ref, total_ref, mixed_ref):
    scores = jnp.einsum(
        "pgd,psd->pgs", query_ref[...], key_ref[...], preferred_element_type=jnp.float32
    ) * scale
    slots = lax.broadcasted_iota(jnp.int32, scores.shape, 2)
    usable = slots < filled_ref[...]
    top = jnp.max(jnp.where(usable, scores, -jnp.inf), axis=-1, keepdims=True)
    weights = jnp.where(usable, jnp.exp(scores - top), 0.0)
    top_ref[...] = jnp.broadcast_to(top, scores.shape)
    total_ref[...] = jnp.broadcast_to(jnp.sum(weights, axis=-1, keepdims=True), scores.shape)
    mixed_ref[...] = jnp.einsum(
        "pgs,psd->pgd",
        weights.astype(jnp.bfloat16),
        value_ref[...],
        preferred_element_type=jnp.float32,
    )


def page_attention(page_queries, keys, values, filled):
    pool_pages, group_count, head_dim = page_queries.shape
    page_slots = keys.shape[1]
    chunk = next(c for c in (32, 16, 8, 4, 2, 1) if pool_pages % c == 0)
    fills = jnp.broadcast_to(filled[:, None, None], (pool_pages, 1, page_slots))
    small = pl.BlockSpec((chunk, group_count, page_slots), lambda i: (i, 0, 0))
    wide = pl.BlockSpec((chunk, group_count, head_dim), lambda i: (i, 0, 0))
    cache = pl.BlockSpec((chunk, page_slots, head_dim), lambda i: (i, 0, 0))
    stat = jax.ShapeDtypeStruct((pool_pages, group_count, page_slots), jnp.float32)
    return pl.pallas_call(
        functools.partial(page_kernel, head_dim ** (-0.5)),
        grid=(pool_pages // chunk,),
        in_specs=[pl.BlockSpec((chunk, 1, page_slots), lambda i: (i, 0, 0)), wide, cache, cache],
        out_specs=[small, small, wide],
        out_shape=[stat, stat, jax.ShapeDtypeStruct(page_queries.shape, jnp.float32)],
        compiler_params=pltpu.CompilerParams(vmem_limit_bytes=24 * 1024 * 1024),
    )(fills, page_queries, keys, values)


def attend(queries, key_cache, value_cache, lengths, page_table):
    req_count, single_head, group_count, head_dim = queries.shape
    pool_pages, single_kv, page_slots, key_dim = key_cache.shape
    owned, filled = page_owners(lengths, page_table, pool_pages, page_slots)
    spread = owned.astype(jnp.bfloat16)
    page_queries = jnp.einsum(
        "rp,rx->px",
        spread,
        queries.reshape(req_count, group_count * head_dim),
        preferred_element_type=jnp.float32,
    ).astype(jnp.bfloat16)
    top, total, mixed = page_attention(
        page_queries.reshape(pool_pages, group_count, head_dim),
        key_cache.reshape(pool_pages, page_slots, head_dim),
        value_cache.reshape(pool_pages, page_slots, head_dim),
        filled,
    )
    top, total = top[:, :, 0].T, total[:, :, 0].T
    row_top = jnp.max(jnp.where(owned[None], top[:, None, :], -jnp.inf), axis=-1)
    page_top = jnp.sum(jnp.where(owned[None], row_top[:, :, None], 0.0), axis=1)
    factor = jnp.exp(top - page_top)
    denominator = jnp.sum(jnp.where(owned[None], (total * factor)[:, None, :], 0.0), axis=-1)
    scaled = mixed * factor.T[:, :, None]
    high = scaled.astype(jnp.bfloat16)
    low = (scaled - high.astype(jnp.float32)).astype(jnp.bfloat16)
    parts = jnp.concatenate([high, low], axis=0).reshape(2 * pool_pages, group_count * head_dim)
    gathered = jnp.dot(
        jnp.concatenate([spread, spread], axis=1), parts, preferred_element_type=jnp.float32
    ).reshape(req_count, group_count, head_dim)
    return (gathered / denominator.T[:, :, None]).astype(jnp.bfloat16).reshape(
        req_count, group_count * head_dim
    )


def sum_kernel(
    peers, part_ref, residual_ref, gain_ref, stream_ref, normed_ref, outgoing, landed, send_sems, recv_sems
):
    me = lax.axis_index("kvh")
    rows = residual_ref.shape[0]
    barrier = pltpu.get_barrier_semaphore()
    for step in range(1, peers):
        pl.semaphore_signal(
            barrier, inc=1, device_id={"kvh": lax.rem(me + step, peers)}, device_id_type=MESH
        )
    for step in range(1, peers):
        block = pl.multiple_of(lax.rem(me + step, peers) * rows, rows)
        outgoing[step - 1] = part_ref[pl.ds(block, rows), :].astype(jnp.bfloat16)
    pl.semaphore_wait(barrier, peers - 1)
    copies = []
    for step in range(1, peers):
        copy = pltpu.make_async_remote_copy(
            src_ref=outgoing.at[step - 1],
            dst_ref=landed.at[step - 1],
            send_sem=send_sems.at[step - 1],
            recv_sem=recv_sems.at[step - 1],
            device_id={"kvh": lax.rem(me + step, peers)},
            device_id_type=MESH,
        )
        copy.start()
        copies.append(copy)
    stream = residual_ref[...].astype(jnp.float32) + part_ref[pl.ds(pl.multiple_of(me * rows, rows), rows), :]
    for step, copy in enumerate(copies):
        copy.wait()
        stream = stream + landed[step].astype(jnp.float32)
    stream_ref[...] = stream
    inverse_rms = lax.rsqrt(jnp.mean(stream * stream, axis=-1, keepdims=True) + 1e-06)
    normed_ref[...] = (stream * inverse_rms * gain_ref[...].astype(jnp.float32)).astype(jnp.bfloat16)


def summed_stream(part, residual_in, norm_gain, peers):
    rows, width = residual_in.shape
    vmem = pl.BlockSpec(memory_space=pltpu.VMEM)
    return pl.pallas_call(
        functools.partial(sum_kernel, peers),
        in_specs=[vmem] * 3,
        out_specs=[vmem] * 2,
        out_shape=[
            jax.ShapeDtypeStruct((rows, width), jnp.float32),
            jax.ShapeDtypeStruct((rows, width), jnp.bfloat16),
        ],
        scratch_shapes=[
            pltpu.VMEM((peers - 1, rows, width), jnp.bfloat16),
            pltpu.VMEM((peers - 1, rows, width), jnp.bfloat16),
            pltpu.SemaphoreType.DMA((peers - 1,)),
            pltpu.SemaphoreType.DMA((peers - 1,)),
        ],
        compiler_params=pltpu.CompilerParams(
            collective_id=0, has_side_effects=True, vmem_limit_bytes=16 * 1024 * 1024
        ),
    )(part, residual_in, norm_gain.reshape(1, width))


def earlier_count(pair_routes):
    positions = jnp.arange(pair_routes.shape[0], dtype=jnp.int32)
    same_expert = pair_routes[:, None] == pair_routes[None, :]
    before = positions[None, :] < positions[:, None]
    return jnp.sum(same_expert & before, axis=1)


def local(
    queries,
    key_cache,
    value_cache,
    lengths,
    page_table,
    residual_in,
    w_out,
    norm_gain,
    route_logits,
    routes,
    w_gate,
    w_up,
    w_down,
):
    attended = attend(queries, key_cache, value_cache, lengths, page_table)
    part = jnp.dot(attended, w_out, preferred_element_type=jnp.float32)
    stream, normed = summed_stream(part, residual_in, norm_gain, lax.axis_size("kvh"))
    logit_max = jnp.max(route_logits, axis=-1, keepdims=True)
    logit_exp = jnp.exp(route_logits - logit_max)
    gate_weights = logit_exp / jnp.sum(logit_exp, axis=-1, keepdims=True)
    expert_count = lax.axis_size("req") * lax.axis_size("kvh")
    token_count, pick_count = routes.shape
    model_width = normed.shape[1]
    slot_depth = max(2, 2 * token_count * pick_count // expert_count)
    pair_routes = routes.reshape(token_count * pick_count)
    pair_slots = earlier_count(pair_routes)
    target = pair_routes * slot_depth + pair_slots
    slot_ids = jnp.arange(expert_count * slot_depth, dtype=jnp.int32)
    chosen = (target[None, :] == slot_ids[:, None]).reshape(
        expert_count * slot_depth, token_count, pick_count
    )
    send_matrix = jnp.any(chosen, axis=-1).astype(jnp.bfloat16)
    outgoing = jnp.dot(send_matrix, normed, preferred_element_type=jnp.float32).astype(jnp.bfloat16)
    outgoing = outgoing.reshape(expert_count, slot_depth, model_width)
    arrived = lax.all_to_all(outgoing, ("req", "kvh"), split_axis=0, concat_axis=0, tiled=True)
    sources, width_slots, arrived_width = arrived.shape
    flat_rows = arrived.reshape(sources * width_slots, arrived_width)
    gate_part = jnp.dot(flat_rows, w_gate[0], preferred_element_type=jnp.float32)
    up_part = jnp.dot(flat_rows, w_up[0], preferred_element_type=jnp.float32)
    hidden = swish_gate(gate_part, up_part).astype(jnp.bfloat16)
    produced = jnp.dot(hidden, w_down[0], preferred_element_type=jnp.float32).astype(jnp.bfloat16)
    returned = lax.all_to_all(
        produced.reshape(sources, width_slots, arrived_width),
        ("req", "kvh"),
        split_axis=0,
        concat_axis=0,
        tiled=True,
    )
    returned = returned.reshape(expert_count * slot_depth, model_width)
    pick_matrix = (target[:, None] == slot_ids[None, :]).astype(jnp.bfloat16)
    picked = jnp.dot(pick_matrix, returned, preferred_element_type=jnp.float32).reshape(
        token_count, pick_count, model_width
    )
    mixture = jnp.sum(gate_weights[:, :, None] * picked, axis=1)
    return (stream + mixture).astype(jnp.bfloat16)


def solution(mesh):
    in_specs = (
        P("req", "kvh", None, None),
        P("req", "kvh", None, None),
        P("req", "kvh", None, None),
        P("req"),
        P("req", None),
        P(("req", "kvh"), None),
        P("kvh", None),
        P(),
        P(("req", "kvh"), None),
        P(("req", "kvh"), None),
        P(("req", "kvh"), None, None),
        P(("req", "kvh"), None, None),
        P(("req", "kvh"), None, None),
    )
    out_specs = P(("req", "kvh"), None)
    return jax.shard_map(local, mesh=mesh, in_specs=in_specs, out_specs=out_specs, check_vma=False)
```

```python
import functools

import jax
import jax.numpy as jnp
from jax import lax
from jax.experimental import pallas as pl
from jax.experimental.pallas import tpu as pltpu
from jax.sharding import PartitionSpec as P

MESH = pl.DeviceIdType.MESH


def swish_gate(gate_part, up_part):
    return gate_part / (1.0 + jnp.exp(-gate_part)) * up_part


def page_owners(lengths, page_table, pool_pages, page_slots):
    entry_count = page_table.shape[1]
    columns = jnp.arange(entry_count, dtype=jnp.int32)
    pool_ids = jnp.arange(pool_pages, dtype=jnp.int32)
    room = lengths[:, None] - columns[None, :] * page_slots
    counts = jnp.clip(room, 0, page_slots)
    matched = page_table[:, :, None] == pool_ids[None, None, :]
    fill = jnp.sum(jnp.where(matched, counts[:, :, None], 0), axis=1)
    return fill > 0, jnp.sum(fill, axis=0)


def page_kernel(scale, filled_ref, query_ref, key_ref, value_ref, top_ref, total_ref, mixed_ref):
    scores = jnp.einsum(
        "pgd,psd->pgs", query_ref[...], key_ref[...], preferred_element_type=jnp.float32
    ) * scale
    slots = lax.broadcasted_iota(jnp.int32, scores.shape, 2)
    usable = slots < filled_ref[...]
    top = jnp.max(jnp.where(usable, scores, -jnp.inf), axis=-1, keepdims=True)
    weights = jnp.where(usable, jnp.exp(scores - top), 0.0)
    top_ref[...] = jnp.broadcast_to(top, scores.shape)
    total_ref[...] = jnp.broadcast_to(jnp.sum(weights, axis=-1, keepdims=True), scores.shape)
    mixed_ref[...] = jnp.einsum(
        "pgs,psd->pgd",
        weights.astype(jnp.bfloat16),
        value_ref[...],
        preferred_element_type=jnp.float32,
    )


def page_attention(page_queries, keys, values, filled):
    pool_pages, group_count, head_dim = page_queries.shape
    page_slots = keys.shape[1]
    chunk = next(c for c in (32, 16, 8, 4, 2, 1) if pool_pages % c == 0)
    fills = jnp.broadcast_to(filled[:, None, None], (pool_pages, 1, page_slots))
    small = pl.BlockSpec((chunk, group_count, page_slots), lambda i: (i, 0, 0))
    wide = pl.BlockSpec((chunk, group_count, head_dim), lambda i: (i, 0, 0))
    cache = pl.BlockSpec((chunk, page_slots, head_dim), lambda i: (i, 0, 0))
    stat = jax.ShapeDtypeStruct((pool_pages, group_count, page_slots), jnp.float32)
    return pl.pallas_call(
        functools.partial(page_kernel, head_dim ** (-0.5)),
        grid=(pool_pages // chunk,),
        in_specs=[pl.BlockSpec((chunk, 1, page_slots), lambda i: (i, 0, 0)), wide, cache, cache],
        out_specs=[small, small, wide],
        out_shape=[stat, stat, jax.ShapeDtypeStruct(page_queries.shape, jnp.float32)],
        compiler_params=pltpu.CompilerParams(vmem_limit_bytes=24 * 1024 * 1024),
    )(fills, page_queries, keys, values)


def attend(queries, key_cache, value_cache, lengths, page_table):
    req_count, single_head, group_count, head_dim = queries.shape
    pool_pages, single_kv, page_slots, key_dim = key_cache.shape
    owned, filled = page_owners(lengths, page_table, pool_pages, page_slots)
    spread = owned.astype(jnp.bfloat16)
    page_queries = jnp.einsum(
        "rp,rx->px",
        spread,
        queries.reshape(req_count, group_count * head_dim),
        preferred_element_type=jnp.float32,
    ).astype(jnp.bfloat16)
    top, total, mixed = page_attention(
        page_queries.reshape(pool_pages, group_count, head_dim),
        key_cache.reshape(pool_pages, page_slots, head_dim),
        value_cache.reshape(pool_pages, page_slots, head_dim),
        filled,
    )
    top, total = top[:, :, 0].T, total[:, :, 0].T
    row_top = jnp.max(jnp.where(owned[None], top[:, None, :], -jnp.inf), axis=-1)
    page_top = jnp.sum(jnp.where(owned[None], row_top[:, :, None], 0.0), axis=1)
    factor = jnp.exp(top - page_top)
    denominator = jnp.sum(jnp.where(owned[None], (total * factor)[:, None, :], 0.0), axis=-1)
    scaled = mixed * factor.T[:, :, None]
    high = scaled.astype(jnp.bfloat16)
    low = (scaled - high.astype(jnp.float32)).astype(jnp.bfloat16)
    parts = jnp.concatenate([high, low], axis=0).reshape(2 * pool_pages, group_count * head_dim)
    gathered = jnp.dot(
        jnp.concatenate([spread, spread], axis=1), parts, preferred_element_type=jnp.float32
    ).reshape(req_count, group_count, head_dim)
    return (gathered / denominator.T[:, :, None]).astype(jnp.bfloat16).reshape(
        req_count, group_count * head_dim
    )


def sum_kernel(
    peers, part_ref, residual_ref, gain_ref, stream_ref, normed_ref, outgoing, landed, send_sems, recv_sems
):
    me = lax.axis_index("kvh")
    rows = residual_ref.shape[0]
    barrier = pltpu.get_barrier_semaphore()
    for step in range(1, peers):
        pl.semaphore_signal(
            barrier, inc=1, device_id={"kvh": lax.rem(me + step, peers)}, device_id_type=MESH
        )
    for step in range(1, peers):
        block = pl.multiple_of(lax.rem(me + step, peers) * rows, rows)
        outgoing[step - 1] = part_ref[pl.ds(block, rows), :].astype(jnp.bfloat16)
    pl.semaphore_wait(barrier, peers - 1)
    copies = []
    for step in range(1, peers):
        copy = pltpu.make_async_remote_copy(
            src_ref=outgoing.at[step - 1],
            dst_ref=landed.at[step - 1],
            send_sem=send_sems.at[step - 1],
            recv_sem=recv_sems.at[step - 1],
            device_id={"kvh": lax.rem(me + step, peers)},
            device_id_type=MESH,
        )
        copy.start()
        copies.append(copy)
    stream = residual_ref[...].astype(jnp.float32) + part_ref[pl.ds(pl.multiple_of(me * rows, rows), rows), :]
    for step, copy in enumerate(copies):
        copy.wait()
        stream = stream + landed[step].astype(jnp.float32)
    stream_ref[...] = stream
    inverse_rms = lax.rsqrt(jnp.mean(stream * stream, axis=-1, keepdims=True) + 1e-06)
    normed_ref[...] = (stream * inverse_rms * gain_ref[...].astype(jnp.float32)).astype(jnp.bfloat16)


def summed_stream(part, residual_in, norm_gain, peers):
    rows, width = residual_in.shape
    vmem = pl.BlockSpec(memory_space=pltpu.VMEM)
    return pl.pallas_call(
        functools.partial(sum_kernel, peers),
        in_specs=[vmem] * 3,
        out_specs=[vmem] * 2,
        out_shape=[
            jax.ShapeDtypeStruct((rows, width), jnp.float32),
            jax.ShapeDtypeStruct((rows, width), jnp.bfloat16),
        ],
        scratch_shapes=[
            pltpu.VMEM((peers - 1, rows, width), jnp.bfloat16),
            pltpu.VMEM((peers - 1, rows, width), jnp.bfloat16),
            pltpu.SemaphoreType.DMA((peers - 1,)),
            pltpu.SemaphoreType.DMA((peers - 1,)),
        ],
        compiler_params=pltpu.CompilerParams(
            collective_id=0, has_side_effects=True, vmem_limit_bytes=16 * 1024 * 1024
        ),
    )(part, residual_in, norm_gain.reshape(1, width))


def earlier_count(pair_routes):
    positions = jnp.arange(pair_routes.shape[0], dtype=jnp.int32)
    same_expert = pair_routes[:, None] == pair_routes[None, :]
    before = positions[None, :] < positions[:, None]
    return jnp.sum(same_expert & before, axis=1)


def local(
    queries,
    key_cache,
    value_cache,
    lengths,
    page_table,
    residual_in,
    w_out,
    norm_gain,
    route_logits,
    routes,
    w_gate,
    w_up,
    w_down,
):
    attended = attend(queries, key_cache, value_cache, lengths, page_table)
    part = jnp.dot(attended, w_out, preferred_element_type=jnp.float32)
    stream, normed = summed_stream(part, residual_in, norm_gain, lax.axis_size("kvh"))
    logit_max = jnp.max(route_logits, axis=-1, keepdims=True)
    logit_exp = jnp.exp(route_logits - logit_max)
    gate_weights = logit_exp / jnp.sum(logit_exp, axis=-1, keepdims=True)
    expert_count = lax.axis_size("req") * lax.axis_size("kvh")
    token_count, pick_count = routes.shape
    model_width = normed.shape[1]
    slot_depth = max(2, 2 * token_count * pick_count // expert_count)
    pair_routes = routes.reshape(token_count * pick_count)
    pair_slots = earlier_count(pair_routes)
    target = pair_routes * slot_depth + pair_slots
    slot_ids = jnp.arange(expert_count * slot_depth, dtype=jnp.int32)
    axes = ("req", "kvh")
    all_routes = lax.all_gather(routes, axes, axis=0, tiled=True)
    mine = lax.axis_index("req") * lax.axis_size("kvh") + lax.axis_index("kvh")
    named = jnp.any(all_routes == mine, axis=-1).reshape(expert_count, token_count)
    tokens = jnp.arange(token_count, dtype=jnp.int32)
    earlier = named[:, None, :] & (tokens[None, None, :] < tokens[None, :, None])
    rank = jnp.sum(earlier.astype(jnp.int32), axis=-1)
    place = jnp.arange(expert_count, dtype=jnp.int32)[:, None] * slot_depth + rank
    place = jnp.where(named, place, -1).reshape(expert_count * token_count)
    take = (place[None, :] == slot_ids[:, None]).astype(jnp.bfloat16)
    all_normed = lax.all_gather(normed, axes, axis=0, tiled=True)
    flat_rows = jnp.dot(take, all_normed, preferred_element_type=jnp.float32).astype(jnp.bfloat16)
    sources, width_slots, arrived_width = expert_count, slot_depth, model_width
    gate_part = jnp.dot(flat_rows, w_gate[0], preferred_element_type=jnp.float32)
    up_part = jnp.dot(flat_rows, w_up[0], preferred_element_type=jnp.float32)
    hidden = swish_gate(gate_part, up_part).astype(jnp.bfloat16)
    produced = jnp.dot(hidden, w_down[0], preferred_element_type=jnp.float32).astype(jnp.bfloat16)
    returned = lax.all_to_all(
        produced.reshape(sources, width_slots, arrived_width),
        ("req", "kvh"),
        split_axis=0,
        concat_axis=0,
        tiled=True,
    )
    returned = returned.reshape(expert_count * slot_depth, model_width)
    pick_matrix = (target[:, None] == slot_ids[None, :]).astype(jnp.bfloat16)
    picked = jnp.dot(pick_matrix, returned, preferred_element_type=jnp.float32).reshape(
        token_count, pick_count, model_width
    )
    mixture = jnp.sum(gate_weights[:, :, None] * picked, axis=1)
    return (stream + mixture).astype(jnp.bfloat16)


def solution(mesh):
    in_specs = (
        P("req", "kvh", None, None),
        P("req", "kvh", None, None),
        P("req", "kvh", None, None),
        P("req"),
        P("req", None),
        P(("req", "kvh"), None),
        P("kvh", None),
        P(),
        P(("req", "kvh"), None),
        P(("req", "kvh"), None),
        P(("req", "kvh"), None, None),
        P(("req", "kvh"), None, None),
        P(("req", "kvh"), None, None),
    )
    out_specs = P(("req", "kvh"), None)
    return jax.shard_map(local, mesh=mesh, in_specs=in_specs, out_specs=out_specs, check_vma=False)
```
